32 devices in a mesh: row: 4 (over y, x), col: 8 (over z, core).
Axes of the slice: x: 2, y: 2, z: 4, core: 2. Of those that a mesh axis runs over, the one named last changes fastest.
Arguments:
- matrix: float32 [4096, 4, 2048], P('row', None, 'col'), may hold values from -28 to 28
Outputs:
- coefficients: float32 [512, 4, 2048], P(None, None, 'col')
- remainder: float32 [4096, 4, 2048], P('row', None, 'col')
The draws below stay inside these ranges and needn't reach their ends.
All inputs are finite; a program needn't handle non-finite values.
Results may differ from the reference program's by a relative error of at most 0.0003.
Values sent between devices are 32-bit elements; how exact they have to be, the bound alone decides.
A program may use at most 64 MiB of HBM per device.

```python
import jax
import jax.numpy as jnp
from jax import lax

BLOCK = 256
NBL = 4
ROWS = 4096
SPAN = 2048


def draw_matrix(key, part):
    first = jax.random.fold_in(key, 0)
    shape = (ROWS, NBL, SPAN)
    return jax.random.truncated_normal(first, -4.0, 4.0, shape, jnp.float32)


def setup_inputs(seed: int = 0) -> dict:
    keys = jax.random.split(jax.random.key(seed), 2)
    matrix = draw_matrix(jax.random.fold_in(keys[1], 71), 0)
    return {"matrix": matrix}


def reference(matrix):
    total_rows = matrix.shape[0]
    flat = matrix.reshape(total_rows, -1)
    panel = flat[:, :2 * BLOCK]
    factor, upper = jnp.linalg.qr(panel)
    signs = jnp.sign(jnp.diagonal(upper))
    factor = factor * signs[None, :]
    coefficients = jnp.dot(factor.T.astype(jnp.float32), flat.astype(jnp.float32), precision=lax.Precision.HIGHEST, preferred_element_type=jnp.float32)
    remainder = flat - jnp.dot(factor.astype(jnp.float32), coefficients.astype(jnp.float32), precision=lax.Precision.HIGHEST, preferred_element_type=jnp.float32)
    return (coefficients.reshape(2 * BLOCK, NBL, SPAN), remainder.reshape(matrix.shape))
```

```python
import functools

import jax
import jax.numpy as jnp
from jax import lax
from jax.experimental import pallas as pl
from jax.experimental.pallas import tpu as pltpu
from jax.sharding import PartitionSpec as P

HIGH = lax.Precision.HIGH
HIGHEST = lax.Precision.HIGHEST
MESH = pl.DeviceIdType.MESH
PIECES = 4
UNITS = 2


def dot_t(a, b, precision):
    return lax.dot_general(
        a, b, (((0,), (0,)), ((), ())), precision=precision, preferred_element_type=jnp.float32
    )


def dot(a, b, precision):
    return jnp.dot(a, b, precision=precision, preferred_element_type=jnp.float32)


def exchange_kernel(
    rows_n, cols_n, a_hbm, panel, red, gram,
    a_v, part, rbuf, load_sem, pload_sem, zs, zr, ss, sr, gzs, gzr, gss, gsr, rs_s, rs_r, ag_s, ag_r,
):
    row = lax.axis_index("row")
    col = lax.axis_index("col")
    chips = cols_n // 2
    bits = rows_n.bit_length() - 1
    z, core = col // 2, col % 2
    sibling = (row, col + 1 - 2 * core)
    above = (row, jnp.minimum(col + 2, cols_n - 1))
    first, last = z == 0, z == chips - 1
    count, nbl, width = a_hbm.shape
    half = width // 2
    step = count // PIECES
    lanes = nbl * width // UNITS
    per_unit = nbl // UNITS

    def partner(b):
        bit = (row // (1 << b)) % 2
        return bit, (row + (1 << b) * (1 - 2 * bit), col)

    loads = [
        pltpu.make_async_copy(a_hbm.at[:, l, :], a_v.at[l], load_sem.at[l]) for l in range(nbl)
    ]
    ploads = [
        pltpu.make_async_copy(
            a_hbm.at[:, 0, h * half : (h + 1) * half], panel.at[h, core], pload_sem.at[h]
        )
        for h in range(2)
    ]

    @pl.when(first)
    def _():
        for c in ploads:
            c.start()

    for c in loads:
        c.start()

    barrier = pltpu.get_barrier_semaphore()
    pl.semaphore_signal(barrier, inc=1, device_id=sibling, device_id_type=MESH)
    for b in range(bits):
        pl.semaphore_signal(barrier, inc=1, device_id=partner(b)[1], device_id_type=MESH)

    @pl.when(jnp.logical_not(first))
    def _():
        pl.semaphore_signal(barrier, inc=1, device_id=(row, col - 2), device_id_type=MESH)

    @pl.when(jnp.logical_not(last))
    def _():
        pl.semaphore_signal(barrier, inc=1, device_id=(row, col + 2), device_id_type=MESH)

    pl.semaphore_wait(
        barrier,
        1 + bits + jnp.where(first, 0, 1) + jnp.where(last, 0, 1),
    )

    def chain(ref, i, zs, zr, ss, sr):
        up = pltpu.make_async_remote_copy(
            src_ref=ref, dst_ref=ref, send_sem=zs.at[i], recv_sem=zr.at[i],
            device_id=above, device_id_type=MESH,
        )
        side = pltpu.make_async_remote_copy(
            src_ref=ref, dst_ref=ref, send_sem=ss.at[i], recv_sem=sr.at[i],
            device_id=sibling, device_id_type=MESH,
        )
        return up, side

    def pieces(h):
        return [
            chain(panel.at[h, core, pl.ds(q * step, step), :], h * PIECES + q, zs, zr, ss, sr)
            for q in range(PIECES)
        ]

    def forward(piece):
        up, side = piece

        @pl.when(jnp.logical_not(first))
        def _():
            up.wait_recv()

        @pl.when(jnp.logical_not(last))
        def _():
            up.start()

        side.start()

    def finish(piece):
        up, side = piece

        @pl.when(jnp.logical_not(last))
        def _():
            up.wait_send()

        side.wait_send()

    def make_unit(h, u):
        lane = pl.ds(u * lanes, lanes)
        k = h * UNITS + u
        tracks = []
        for s in range(2):
            order = [(i + s * (bits // 2)) % bits for i in range(bits)]
            start, size, off = s * half, half, 0
            down = []
            for i, b in enumerate(order):
                bit, dev = partner(b)
                size //= 2
                keep = pl.multiple_of(start + bit * size, 8)
                send = pl.multiple_of(start + (1 - bit) * size, 8)
                buf = rbuf.at[k, s, pl.ds(off, size), :]
                copy = pltpu.make_async_remote_copy(
                    src_ref=part.at[h, pl.ds(send, size), lane], dst_ref=buf,
                    send_sem=rs_s.at[k, s, i], recv_sem=rs_r.at[k, s, i],
                    device_id=dev, device_id_type=MESH,
                )
                down.append((copy, keep, size, off, start))
                start, off = keep, off + size
            up = []
            for i in reversed(range(bits)):
                _, keep, size, _, _ = down[i]
                region = red.at[h, pl.ds(keep, size), lane]
                up.append(
                    pltpu.make_async_remote_copy(
                        src_ref=region, dst_ref=region,
                        send_sem=ag_s.at[k, s, i], recv_sem=ag_r.at[k, s, i],
                        device_id=partner(order[i])[1], device_id_type=MESH,
                    )
                )
            tracks.append((s, down, up))
        return h, lane, k, tracks

    def unit_events(unit):
        h, lane, k, tracks = unit

        def rs_step(i):
            for s, down, up in tracks:
                copy, keep, size, off, _ = down[i]
                copy.wait_recv()
                total = part[h, pl.ds(keep, size), lane] + rbuf[k, s, pl.ds(off, size), :]
                if i + 1 < bits:
                    part[h, pl.ds(keep, size), lane] = total
                    down[i + 1][0].start()
                else:
                    red[h, pl.ds(keep, size), lane] = total
                    up[0].start()

        def ag_step(i):
            for s, down, up in tracks:
                up[i].wait_recv()
                if i + 1 < bits:
                    up[i + 1].start()

        return [functools.partial(rs_step, i) for i in range(bits)] + [
            functools.partial(ag_step, i) for i in range(bits)
        ]

    def multiply(h, u):
        left = jnp.concatenate([panel[h, 0], panel[h, 1]], axis=1)
        for l in range(u * per_unit, (u + 1) * per_unit):
            part[h, :, l * width : (l + 1) * width] = dot_t(left, a_v[l], HIGH)

    def begin(unit):
        for s, down, up in unit[3]:
            down[0][0].start()

    all_pieces = [pieces(0), pieces(1)]
    units = [[make_unit(h, u) for u in range(UNITS)] for h in range(2)]
    events = [[unit_events(u) for u in units[h]] for h in range(2)]

    @pl.when(first)
    def _():
        ploads[0].wait()

    for p in all_pieces[0]:
        forward(p)

    @pl.when(first)
    def _():
        ploads[1].wait()

    for c in loads:
        c.wait()
    for p in all_pieces[0]:
        p[1].wait_recv()
    for u in range(UNITS):
        multiply(0, u)
        begin(units[0][u])
    queue = [e for group in zip(*events[0]) for e in group]
    for i, p in enumerate(all_pieces[1]):
        forward(p)
        if i >= 1 and queue:
            queue.pop(0)()
    for p in all_pieces[1]:
        p[1].wait_recv()
    for u in range(UNITS):
        multiply(1, u)
        begin(units[1][u])
        if queue:
            queue.pop(0)()
    later = [e for group in zip(*events[1]) for e in group]
    n = max(len(queue), len(later))
    while queue or later:
        if queue:
            queue.pop(0)()
        if later and len(later) >= len(queue):
            later.pop(0)()

    @pl.when(first)
    def _():
        for b in range(2):
            for h in range(2):
                gram[core, pl.ds((2 * b + h) * half, half), :] = red[h, b * half : (b + 1) * half, :width]

    gpieces = [
        chain(gram.at[core, pl.ds(q * half, half), :], q, gzs, gzr, gss, gsr) for q in range(4)
    ]
    for p in gpieces:
        forward(p)
    for p in gpieces:
        p[1].wait_recv()
    for p in all_pieces[0] + all_pieces[1] + gpieces:
        finish(p)
    for h in range(2):
        for unit in units[h]:
            for s, down, up in unit[3]:
                for d in down:
                    d[0].wait_send()
                for c in up:
                    c.wait_send()


def exchange(mesh, matrix):
    rows_n, cols_n = mesh.shape["row"], mesh.shape["col"]
    bits = rows_n.bit_length() - 1
    count, nbl, width = matrix.shape
    half = width // 2
    f32 = jnp.float32
    dma = pltpu.SemaphoreType.DMA
    vmem = pl.BlockSpec(memory_space=pltpu.VMEM)
    return pl.pallas_call(
        functools.partial(exchange_kernel, rows_n, cols_n),
        out_shape=(
            jax.ShapeDtypeStruct((2, 2, count, half), f32),
            jax.ShapeDtypeStruct((2, width, nbl * width), f32),
            jax.ShapeDtypeStruct((2, 2 * width, width), f32),
        ),
        in_specs=[pl.BlockSpec(memory_space=pl.ANY)],
        out_specs=(vmem, vmem, vmem),
        scratch_shapes=[
            pltpu.VMEM((nbl, count, width), f32),
            pltpu.VMEM((2, width, nbl * width), f32),
            pltpu.VMEM((2 * UNITS, 2, half, nbl * width // UNITS), f32),
            dma((nbl,)),
            dma((2,)),
        ]
        + [dma((2 * PIECES,))] * 4
        + [dma((4,))] * 4
        + [dma((2 * UNITS, 2, bits))] * 4,
        compiler_params=pltpu.CompilerParams(
            collective_id=0, has_side_effects=True, vmem_limit_bytes=48 * 1024 * 1024
        ),
        name="exchange",
    )(matrix)


def factor_block(sref, uref, size):
    def panel_step(p, carry):
        base = pl.multiple_of(p * 8, 8)
        rows = sref[pl.ds(base, 8), :]
        near = pltpu.roll(rows[:, :size], (size - base) % size, 1)
        e = {}
        for i in range(8):
            for k in range(i, 8):
                e[i, k] = jnp.broadcast_to(near[i : i + 1, k : k + 1], (1, size))
        s = [rows[i : i + 1, :] for i in range(8)]
        us = []
        for j in range(8):
            d = e[j, j]
            r = lax.rsqrt(d)
            r = r * (1.5 - 0.5 * (d * r) * r)
            f = {k: e[j, k] * r for k in range(j + 1, 8)}
            for i in range(j + 1, 8):
                for k in range(i, 8):
                    e[i, k] = e[i, k] - f[i] * f[k]
            u = s[j] * jnp.concatenate([r, r], axis=1)
            us.append(u)
            for i in range(j + 1, 8):
                s[i] = s[i] - jnp.concatenate([f[i], f[i]], axis=1) * u
        u8 = jnp.concatenate(us, axis=0)
        uref[pl.ds(base, 8), :] = u8
        sref[...] = sref[...] - dot_t(u8[:, :size], u8, HIGHEST)
        return carry

    lax.fori_loop(0, size // 8, panel_step, 0)


def finish_kernel(a_hbm, panel, red, gram, coef_hbm, rem_hbm, a_v, s_v, m_v, sref, uref, w_v, c_v, x_v, out_v, load_sem, c_sem, r_sem):
    count, nbl, width = a_hbm.shape
    half = width // 2
    n = 2 * width
    loads = [
        pltpu.make_async_copy(a_hbm.at[:, l, :], a_v.at[l], load_sem.at[l]) for l in range(nbl)
    ]
    for c in loads:
        c.start()
    s_v[:, :width] = gram[0]
    s_v[:, width:] = gram[1]
    eye_n = lax.broadcasted_iota(jnp.int32, (n, n), 0) == lax.broadcasted_iota(jnp.int32, (n, n), 1)
    m_v[...] = jnp.where(eye_n, 1.0, 0.0)
    eye = jnp.where(
        lax.broadcasted_iota(jnp.int32, (half, half), 0) == lax.broadcasted_iota(jnp.int32, (half, half), 1),
        1.0, 0.0,
    )
    lower = lax.broadcasted_iota(jnp.int32, (half, half), 0) >= lax.broadcasted_iota(jnp.int32, (half, half), 1)
    blocks = n // half
    for b in range(blocks):
        lo, hi = b * half, (b + 1) * half
        sref[:, :half] = s_v[lo:hi, lo:hi]
        sref[:, half:] = eye
        factor_block(sref, uref, half)
        inv = jnp.where(lower, uref[:, half:], 0.0)
        if b == 0:
            m_v[lo:hi, :hi] = inv
        else:
            m_v[lo:hi, :lo] = dot(inv, m_v[lo:hi, :lo], HIGHEST)
            m_v[lo:hi, lo:hi] = inv
        if hi < n:
            u = dot(inv, s_v[lo:hi, hi:], HIGHEST)
            s_v[hi:, hi:] = s_v[hi:, hi:] - dot_t(u, u, HIGHEST)
            m_v[hi:, :hi] = m_v[hi:, :hi] - dot_t(u, m_v[lo:hi, :hi], HIGHEST)
    for h in range(2):
        for b in range(2):
            w_v[(2 * b + h) * half : (2 * b + h + 1) * half, :] = red[h, b * half : (b + 1) * half, :]
    outs = []
    for l in range(nbl):
        at = slice(l * width, (l + 1) * width)
        c_v[l] = dot(m_v[...], w_v[:, at], HIGH)
        copy = pltpu.make_async_copy(c_v.at[l], coef_hbm.at[:, l, :], c_sem.at[l])
        copy.start()
        outs.append(copy)
    for l in range(nbl):
        loads[l].wait()
        x_v[...] = dot_t(m_v[...], c_v[l], HIGH)
        total = a_v[l]
        for h in range(2):
            for b in range(2):
                at = (2 * b + h) * half
                total = total - dot(panel[h, b], x_v[at : at + half, :], HIGH)
        out_v[l] = total
        copy = pltpu.make_async_copy(out_v.at[l], rem_hbm.at[:, l, :], r_sem.at[l])
        copy.start()
        outs.append(copy)
    for c in outs:
        c.wait()


def finish(matrix, panel, red, gram):
    count, nbl, width = matrix.shape
    half, n = width // 2, 2 * width
    f32 = jnp.float32
    dma = pltpu.SemaphoreType.DMA
    vmem = pl.BlockSpec(memory_space=pltpu.VMEM)
    anywhere = pl.BlockSpec(memory_space=pl.ANY)
    return pl.pallas_call(
        finish_kernel,
        out_shape=(
            jax.ShapeDtypeStruct((n, nbl, width), f32),
            jax.ShapeDtypeStruct((count, nbl, width), f32),
        ),
        in_specs=[anywhere, vmem, vmem, vmem],
        out_specs=(anywhere, anywhere),
        scratch_shapes=[
            pltpu.VMEM((nbl, count, width), f32),
            pltpu.VMEM((n, n), f32),
            pltpu.VMEM((n, n), f32),
            pltpu.VMEM((half, width), f32),
            pltpu.VMEM((half, width), f32),
            pltpu.VMEM((n, nbl * width), f32),
            pltpu.VMEM((nbl, n, width), f32),
            pltpu.VMEM((n, width), f32),
            pltpu.VMEM((nbl, count, width), f32),
            dma((nbl,)),
            dma((nbl,)),
            dma((nbl,)),
        ],
        compiler_params=pltpu.CompilerParams(vmem_limit_bytes=48 * 1024 * 1024),
        name="finish",
    )(matrix, panel, red, gram)


def solution(mesh):
    def on_device(matrix):
        panel, red, gram = exchange(mesh, matrix)
        return finish(matrix, panel, red, gram)

    return jax.shard_map(
        on_device,
        mesh=mesh,
        in_specs=(P("row", None, "col"),),
        out_specs=(P(None, None, "col"), P("row", None, "col")),
        check_vma=False,
    )
```

```python
import functools

import jax
import jax.numpy as jnp
from jax import lax
from jax.experimental import pallas as pl
from jax.experimental.pallas import tpu as pltpu
from jax.sharding import PartitionSpec as P

HIGH = lax.Precision.HIGH
HIGHEST = lax.Precision.HIGHEST
MESH = pl.DeviceIdType.MESH
PIECES = 4
PANEL = 16


def dot_t(a, b, precision):
    return lax.dot_general(
        a, b, (((0,), (0,)), ((), ())), precision=precision, preferred_element_type=jnp.float32
    )


def dot(a, b, precision):
    return jnp.dot(a, b, precision=precision, preferred_element_type=jnp.float32)


def dot_nt(a, b, precision):
    return lax.dot_general(
        a, b, (((1,), (1,)), ((), ())), precision=precision, preferred_element_type=jnp.float32
    )


def factor_panels(sref, uref, size, begin, end):
    def panel_step(p, carry):
        base = pl.multiple_of(p * PANEL, PANEL)
        rows = sref[pl.ds(base, PANEL), :]
        near = pltpu.roll(rows[:, :size], lax.rem(size - base, size), 1)
        e = {}
        for i in range(PANEL):
            for k in range(i, PANEL):
                e[i, k] = jnp.broadcast_to(near[i : i + 1, k : k + 1], (1, size))
        s = [[rows[i : i + 1, :size], rows[i : i + 1, size:]] for i in range(PANEL)]
        us = []
        for j in range(PANEL):
            d = e[j, j]
            inv = pl.reciprocal(d, approx=True)
            root = lax.rsqrt(d)
            us.append(jnp.concatenate([s[j][0] * root, s[j][1] * root], axis=1))
            if j + 1 < PANEL:
                square = e[j, j + 1] * e[j, j + 1]
                e[j + 1, j + 1] = e[j + 1, j + 1] - square * inv
            for i in range(j + 1, PANEL):
                t = e[j, i] * inv
                for k in range(i, PANEL):
                    if (i, k) != (j + 1, j + 1):
                        e[i, k] = e[i, k] - t * e[j, k]
                s[i] = [s[i][0] - t * s[j][0], s[i][1] - t * s[j][1]]
        u = jnp.concatenate(us, axis=0)
        uref[pl.ds(base, PANEL), :] = u
        sref[...] = sref[...] - dot_t(u[:, :size], u, HIGHEST)
        return carry

    lax.fori_loop(begin, end, panel_step, 0)


def qr_kernel(
    rows_n, cols_n, a_hbm, coef_hbm, rem_hbm,
    a_v, panel, part, red, rbuf, gram, s_v, m_v, sref, uref, c_v,
    load_sem, pload_sem, c_sem, r_sem,
    zs, zr, ss, sr, mzs, mzr, mss, msr, gss, gsr, rs_s, rs_r, ag_s, ag_r,
):
    row = lax.axis_index("row")
    col = lax.axis_index("col")
    chips = cols_n // 2
    bits = rows_n.bit_length() - 1
    z, core = col // 2, col % 2
    sibling = (row, col + 1 - 2 * core)
    above = (row, jnp.minimum(col + 2, cols_n - 1))
    first, last = z == 0, z == chips - 1
    later = jnp.logical_not(first)
    inner = jnp.logical_not(last)
    count, nbl, width = a_hbm.shape
    half = width // 2
    n = 2 * width
    blocks = n // half
    step = count // PIECES

    def partner(b):
        bit = (row // (1 << b)) % 2
        return bit, (row + (1 << b) * (1 - 2 * bit), col)

    loads = [
        pltpu.make_async_copy(a_hbm.at[:, l, :], a_v.at[l], load_sem.at[l]) for l in range(nbl)
    ]
    ploads = [
        pltpu.make_async_copy(
            a_hbm.at[:, 0, h * half : (h + 1) * half], panel.at[2 * core + h], pload_sem.at[h]
        )
        for h in range(2)
    ]

    @pl.when(first)
    def _():
        for c in ploads:
            c.start()

    for c in loads:
        c.start()

    barrier = pltpu.get_barrier_semaphore()
    pl.semaphore_signal(barrier, inc=1, device_id=sibling, device_id_type=MESH)
    for b in range(bits):
        pl.semaphore_signal(barrier, inc=1, device_id=partner(b)[1], device_id_type=MESH)

    @pl.when(later)
    def _():
        pl.semaphore_signal(barrier, inc=1, device_id=(row, col - 2), device_id_type=MESH)

    @pl.when(inner)
    def _():
        pl.semaphore_signal(barrier, inc=1, device_id=(row, col + 2), device_id_type=MESH)

    pl.semaphore_wait(barrier, 1 + bits + jnp.where(first, 0, 1) + jnp.where(last, 0, 1))

    def chain(ref, i, zs, zr, ss, sr):
        up = pltpu.make_async_remote_copy(
            src_ref=ref, dst_ref=ref, send_sem=zs.at[i], recv_sem=zr.at[i],
            device_id=above, device_id_type=MESH,
        )
        side = pltpu.make_async_remote_copy(
            src_ref=ref, dst_ref=ref, send_sem=ss.at[i], recv_sem=sr.at[i],
            device_id=sibling, device_id_type=MESH,
        )
        return up, side

    def forward(piece):
        up, side = piece
        up.wait_recv()

        @pl.when(inner)
        def _():
            up.start()

        side.start()

    pieces = [
        [
            chain(panel.at[2 * core + h, pl.ds(q * step, step), :], h * PIECES + q, zs, zr, ss, sr)
            for q in range(PIECES)
        ]
        for h in range(2)
    ]
    quarter = half // 4
    mpieces = [
        [
            chain(
                m_v.at[
                    pl.ds(pl.multiple_of(b * half + core * 2 * quarter + q * quarter, 8), quarter),
                    pl.ds(0, (b + 1) * half),
                ],
                2 * b + q, mzs, mzr, mss, msr,
            )
            for q in range(2)
        ]
        for b in range(blocks)
    ]

    def make_unit(h, l):
        lane = pl.ds(l * width, width)
        k = h * nbl + l
        tracks = []
        for s in range(2):
            order = [(i + s * (bits // 2)) % bits for i in range(bits)]
            start, size, off = (2 * s + h) * half, half, 0
            down = []
            for i, b in enumerate(order):
                bit, dev = partner(b)
                size //= 2
                keep = pl.multiple_of(start + bit * size, 8)
                send = pl.multiple_of(start + (1 - bit) * size, 8)
                copy = pltpu.make_async_remote_copy(
                    src_ref=part.at[pl.ds(send, size), lane],
                    dst_ref=rbuf.at[k, s, pl.ds(off, size), :],
                    send_sem=rs_s.at[k, s, i], recv_sem=rs_r.at[k, s, i],
                    device_id=dev, device_id_type=MESH,
                )
                down.append((copy, keep, size, off))
                start, off = keep, off + size
            up = []
            for i in reversed(range(bits)):
                _, keep, size, _ = down[i]
                region = red.at[pl.ds(keep, size), lane]
                up.append(
                    pltpu.make_async_remote_copy(
                        src_ref=region, dst_ref=region,
                        send_sem=ag_s.at[k, s, i], recv_sem=ag_r.at[k, s, i],
                        device_id=partner(order[i])[1], device_id_type=MESH,
                    )
                )
            tracks.append((s, down, up))
        return lane, k, tracks

    def unit_events(unit):
        lane, k, tracks = unit

        def rs_step(i):
            for s, down, up in tracks:
                copy, keep, size, off = down[i]
                copy.wait_recv()
                total = part[pl.ds(keep, size), lane] + rbuf[k, s, pl.ds(off, size), :]
                if i + 1 < bits:
                    part[pl.ds(keep, size), lane] = total
                    down[i + 1][0].start()
                else:
                    red[pl.ds(keep, size), lane] = total
                    up[0].start()

        def ag_step(i):
            for s, down, up in tracks:
                up[i].wait_recv()
                if i + 1 < bits:
                    up[i + 1].start()

        return [functools.partial(rs_step, i) for i in range(bits)] + [
            functools.partial(ag_step, i) for i in range(bits)
        ]

    def begin(unit):
        for s, down, up in unit[2]:
            down[0][0].start()

    def multiply(h, l):
        left = jnp.concatenate([panel[h], panel[2 + h]], axis=1)
        out = dot_t(left, a_v[l], HIGH)
        for b in range(2):
            part[(2 * b + h) * half : (2 * b + h + 1) * half, l * width : (l + 1) * width] = out[
                b * half : (b + 1) * half
            ]

    units = [[make_unit(h, l) for l in range(nbl)] for h in range(2)]

    def wave(unit_list):
        return [e for group in zip(*[unit_events(u) for u in unit_list]) for e in group]

    def run(queue, number):
        for _ in range(min(number, len(queue))):
            queue.pop(0)()

    def project(lo, hi, finished):
        m = m_v[lo:hi, :hi]
        left = jnp.concatenate([panel[i] for i in range(hi // half)], axis=1)
        q = dot_nt(left, m, HIGH)
        for l in range(nbl):
            at = slice(l * width, (l + 1) * width)
            c = dot(m, red[:hi, at], HIGH)
            c_v[l, lo:hi, :] = c
            a_v[l] = a_v[l] - dot(q, c, HIGH)
            if finished:
                outs[l].start()
                couts[l].start()

    outs = [
        pltpu.make_async_copy(a_v.at[l], rem_hbm.at[:, l, :], r_sem.at[l]) for l in range(nbl)
    ]
    couts = [
        pltpu.make_async_copy(c_v.at[l], coef_hbm.at[:, l, :], c_sem.at[l]) for l in range(nbl)
    ]

    @pl.when(first)
    def _():
        for h in range(2):
            ploads[h].wait()
            for up, side in pieces[h]:
                side.start()
        for h in range(2):
            for up, side in pieces[h]:
                up.start()
        loads[0].wait()
        for h in range(2):
            for up, side in pieces[h]:
                side.wait_recv()
            multiply(h, 0)
            begin(units[h][0])
        queue = wave([units[0][0], units[1][0]])
        for l in range(1, nbl):
            loads[l].wait()
            multiply(0, l)
            multiply(1, l)
            run(queue, 2)
        run(queue, len(queue))
        rest = [units[h][l] for h in range(2) for l in range(1, nbl)]
        for u in rest:
            begin(u)
        gram[core] = red[:, :width]
        side = pltpu.make_async_remote_copy(
            src_ref=gram.at[core], dst_ref=gram.at[core], send_sem=gss.at[0], recv_sem=gsr.at[0],
            device_id=sibling, device_id_type=MESH,
        )
        side.start()
        line = lax.broadcasted_iota(jnp.int32, (half, half), 0)
        lane = lax.broadcasted_iota(jnp.int32, (half, half), 1)
        m_v[...] = jnp.zeros_like(m_v)
        for b in range(blocks):
            at = slice(b * half, (b + 1) * half)
            m_v[at, at] = jnp.where(line == lane, 1.0, 0.0)
        side.wait_recv()
        s_v[:, :width] = gram[0]
        s_v[:, width:] = gram[1]
        queue = wave(rest)
        share = -(-len(queue) // (2 * blocks - 1))
        panels = half // PANEL
        for b in range(blocks):
            lo, hi = b * half, (b + 1) * half
            sref[:, :half] = s_v[lo:hi, lo:hi]
            sref[:, half:] = jnp.where(line == lane, 1.0, 0.0)
            factor_panels(sref, uref, half, 0, panels // 2)
            run(queue, share)
            factor_panels(sref, uref, half, panels // 2, panels)
            inv = jnp.where(line >= lane, uref[:, half:], 0.0)
            if b > 0:
                m_v[lo:hi, :lo] = dot(inv, m_v[lo:hi, :lo], HIGHEST)
            m_v[lo:hi, lo:hi] = inv
            for up, _ in mpieces[b]:
                up.start()
            if hi < n:
                u = dot(inv, s_v[lo:hi, hi:], HIGHEST)
                s_v[hi:, hi:] = s_v[hi:, hi:] - dot_t(u, u, HIGHEST)
                m_v[hi:, :hi] = m_v[hi:, :hi] - dot_t(u, m_v[lo:hi, :hi], HIGHEST)
            run(queue, share)
        run(queue, len(queue))
        project(0, width, False)
        project(width, width + half, False)
        for h in range(2):
            for up, other in pieces[h]:
                up.wait_send()
        for b in range(blocks):
            for up, _ in mpieces[b]:
                up.wait_send()
        side.wait_send()

    @pl.when(later)
    def _():
        m_v[:half, half:width] = jnp.zeros((half, half), jnp.float32)
        for p in pieces[0]:
            forward(p)
        for c in loads:
            c.wait()
        for up, side in pieces[0]:
            side.wait_recv()
        for l in range(nbl):
            multiply(0, l)
            begin(units[0][l])
        queue = wave(units[0])
        for i, p in enumerate(pieces[1]):
            forward(p)
            run(queue, nbl - 1)
        for up, side in pieces[1]:
            side.wait_recv()
        for l in range(nbl):
            multiply(1, l)
            begin(units[1][l])
            run(queue, 1)
        run(queue, len(queue))
        queue = wave(units[1])
        run(queue, nbl * bits)
        for p in mpieces[0]:
            forward(p)
        run(queue, nbl)
        for p in mpieces[1]:
            forward(p)
        run(queue, len(queue))
        for p in mpieces[2]:
            forward(p)

        @pl.when(inner)
        def _():
            for p in mpieces[3]:
                forward(p)

        for b in range(2):
            for up, side in mpieces[b]:
                side.wait_recv()
        project(0, width, False)
        for up, side in mpieces[2]:
            side.wait_recv()
        project(width, width + half, False)

        @pl.when(last)
        def _():
            for p in mpieces[3]:
                forward(p)

        for up, side in mpieces[3]:
            side.wait_recv()
        for group in mpieces:
            for up, side in group:
                side.wait_send()

        @pl.when(inner)
        def _():
            for group in pieces + mpieces:
                for up, side in group:
                    up.wait_send()

    project(width + half, n, True)
    for h in range(2):
        for up, side in pieces[h]:
            side.wait_send()
        for unit in units[h]:
            for s, down, up in unit[2]:
                for d in down:
                    d[0].wait_send()
                for c in up:
                    c.wait_send()
    for c in outs + couts:
        c.wait()


def solution(mesh):
    rows_n, cols_n = mesh.shape["row"], mesh.shape["col"]
    bits = rows_n.bit_length() - 1

    def on_device(matrix):
        count, nbl, width = matrix.shape
        half, n = width // 2, 2 * width
        units = 2 * nbl
        f32 = jnp.float32
        dma = pltpu.SemaphoreType.DMA
        anywhere = pl.BlockSpec(memory_space=pl.ANY)
        return pl.pallas_call(
            functools.partial(qr_kernel, rows_n, cols_n),
            out_shape=(
                jax.ShapeDtypeStruct((n, nbl, width), f32),
                jax.ShapeDtypeStruct((count, nbl, width), f32),
            ),
            in_specs=[anywhere],
            out_specs=(anywhere, anywhere),
            scratch_shapes=[
                pltpu.VMEM((nbl, count, width), f32),
                pltpu.VMEM((n // half, count, half), f32),
                pltpu.VMEM((n, nbl * width), f32),
                pltpu.VMEM((n, nbl * width), f32),
                pltpu.VMEM((units, 2, half, width), f32),
                pltpu.VMEM((2, n, width), f32),
                pltpu.VMEM((n, n), f32),
                pltpu.VMEM((n, n), f32),
                pltpu.VMEM((half, width), f32),
                pltpu.VMEM((half, width), f32),
                pltpu.VMEM((nbl, n, width), f32),
                dma((nbl,)),
                dma((2,)),
                dma((nbl,)),
                dma((nbl,)),
            ]
            + [dma((2 * PIECES,))] * 4
            + [dma((2 * n // half,))] * 4
            + [dma((1,))] * 2
            + [dma((units, 2, bits))] * 4,
            compiler_params=pltpu.CompilerParams(
                collective_id=0, has_side_effects=True, vmem_limit_bytes=48 * 1024 * 1024
            ),
            name="block_qr",
        )(matrix)

    return jax.shard_map(
        on_device,
        mesh=mesh,
        in_specs=(P("row", None, "col"),),
        out_specs=(P(None, None, "col"), P("row", None, "col")),
        check_vma=False,
    )
```

```python
import functools

import jax
import jax.numpy as jnp
from jax import lax
from jax.experimental import pallas as pl
from jax.experimental.pallas import tpu as pltpu
from jax.sharding import PartitionSpec as P

HIGH = lax.Precision.HIGH
MESH = pl.DeviceIdType.MESH
PIECES = 4
PANEL = 8


def dot_t(a, b, precision):
    return lax.dot_general(
        a, b, (((0,), (0,)), ((), ())), precision=precision, preferred_element_type=jnp.float32
    )


def dot(a, b, precision):
    return jnp.dot(a, b, precision=precision, preferred_element_type=jnp.float32)


def dot_nt(a, b, precision):
    return lax.dot_general(
        a, b, (((1,), (1,)), ((), ())), precision=precision, preferred_element_type=jnp.float32
    )


def split(x):
    a = x.astype(jnp.bfloat16).astype(jnp.float32)
    b = (x - a).astype(jnp.bfloat16).astype(jnp.float32)
    c = (x - a - b).astype(jnp.bfloat16).astype(jnp.float32)
    return a, b, c


def stack_left(x, axis):
    a, b, c = split(x)
    return jnp.concatenate([a, a, b, b, a, c], axis=axis).astype(jnp.bfloat16)


def stack_right(x):
    a, b, c = split(x)
    return jnp.concatenate([a, b, a, b, c, a], axis=0).astype(jnp.bfloat16)


def full_t(a, b):
    return dot_t(stack_left(a, 0), stack_right(b), None)


def full(a, b):
    return dot(stack_left(a, 1), stack_right(b), None)


def factor_panels(sref, uref, size, begin, end):
    def panel_step(p, carry):
        base = pl.multiple_of(p * PANEL, PANEL)
        rows = sref[pl.ds(base, PANEL), :]
        near = pltpu.roll(rows[:, :size], lax.rem(size - base, size), 1)
        e = {}
        for i in range(PANEL):
            for k in range(i, PANEL):
                e[i, k] = jnp.broadcast_to(near[i : i + 1, k : k + 1], (1, size))
        s = [[rows[i : i + 1, :size], rows[i : i + 1, size:]] for i in range(PANEL)]
        us = []
        for j in range(PANEL):
            d = e[j, j]
            inv = pl.reciprocal(d, approx=True)
            root = lax.rsqrt(d)
            us.append(jnp.concatenate([s[j][0] * root, s[j][1] * root], axis=1))
            if j + 1 < PANEL:
                square = e[j, j + 1] * e[j, j + 1]
                e[j + 1, j + 1] = e[j + 1, j + 1] - square * inv
            for i in range(j + 1, PANEL):
                t = e[j, i] * inv
                for k in range(i, PANEL):
                    if (i, k) != (j + 1, j + 1):
                        e[i, k] = e[i, k] - t * e[j, k]
                s[i] = [s[i][0] - t * s[j][0], s[i][1] - t * s[j][1]]
        u = jnp.concatenate(us, axis=0)
        uref[pl.ds(base, PANEL), :] = u
        sref[...] = sref[...] - full_t(u[:, :size], u)
        return carry

    lax.fori_loop(begin, end, panel_step, 0)


def qr_kernel(
    rows_n, cols_n, a_hbm, coef_hbm, rem_hbm,
    a_v, panel, part, red, rbuf, gram, s_v, m_v, sref, uref, c_v,
    load_sem, pload_sem, c_sem, r_sem,
    zs, zr, ss, sr, mzs, mzr, mss, msr, gss, gsr, rs_s, rs_r, ag_s, ag_r,
):
    row = lax.axis_index("row")
    col = lax.axis_index("col")
    chips = cols_n // 2
    bits = rows_n.bit_length() - 1
    z, core = col // 2, col % 2
    sibling = (row, col + 1 - 2 * core)
    above = (row, jnp.minimum(col + 2, cols_n - 1))
    first, last = z == 0, z == chips - 1
    later = jnp.logical_not(first)
    inner = jnp.logical_not(last)
    count, nbl, width = a_hbm.shape
    half = width // 2
    n = 2 * width
    blocks = n // half
    step = count // PIECES

    def partner(b):
        bit = (row // (1 << b)) % 2
        return bit, (row + (1 << b) * (1 - 2 * bit), col)

    loads = [
        pltpu.make_async_copy(a_hbm.at[:, l, :], a_v.at[l], load_sem.at[l]) for l in range(nbl)
    ]
    ploads = [
        pltpu.make_async_copy(
            a_hbm.at[:, 0, h * half : (h + 1) * half], panel.at[2 * core + h], pload_sem.at[h]
        )
        for h in range(2)
    ]

    @pl.when(first)
    def _():
        for c in ploads:
            c.start()

    for c in loads:
        c.start()

    barrier = pltpu.get_barrier_semaphore()
    pl.semaphore_signal(barrier, inc=1, device_id=sibling, device_id_type=MESH)
    for b in range(bits):
        pl.semaphore_signal(barrier, inc=1, device_id=partner(b)[1], device_id_type=MESH)

    @pl.when(later)
    def _():
        pl.semaphore_signal(barrier, inc=1, device_id=(row, col - 2), device_id_type=MESH)

    @pl.when(inner)
    def _():
        pl.semaphore_signal(barrier, inc=1, device_id=(row, col + 2), device_id_type=MESH)

    pl.semaphore_wait(barrier, 1 + bits + jnp.where(first, 0, 1) + jnp.where(last, 0, 1))

    def chain(ref, i, zs, zr, ss, sr):
        up = pltpu.make_async_remote_copy(
            src_ref=ref, dst_ref=ref, send_sem=zs.at[i], recv_sem=zr.at[i],
            device_id=above, device_id_type=MESH,
        )
        side = pltpu.make_async_remote_copy(
            src_ref=ref, dst_ref=ref, send_sem=ss.at[i], recv_sem=sr.at[i],
            device_id=sibling, device_id_type=MESH,
        )
        return up, side

    def forward(piece):
        up, side = piece
        up.wait_recv()

        @pl.when(inner)
        def _():
            up.start()

        side.start()

    pieces = [
        [
            chain(panel.at[2 * core + h, pl.ds(q * step, step), :], h * PIECES + q, zs, zr, ss, sr)
            for q in range(PIECES)
        ]
        for h in range(2)
    ]
    quarter = half // 4
    mpieces = [
        [
            chain(
                m_v.at[
                    pl.ds(pl.multiple_of(b * half + core * 2 * quarter + q * quarter, 8), quarter),
                    pl.ds(0, (b + 1) * half),
                ],
                2 * b + q, mzs, mzr, mss, msr,
            )
            for q in range(2)
        ]
        for b in range(blocks)
    ]

    def make_unit(h, l):
        lane = pl.ds(l * width, width)
        k = h * nbl + l
        tracks = []
        for s in range(2):
            order = [(i + s * (bits // 2)) % bits for i in range(bits)]
            start, size, off = (2 * s + h) * half, half, 0
            down = []
            for i, b in enumerate(order):
                bit, dev = partner(b)
                size //= 2
                keep = pl.multiple_of(start + bit * size, 8)
                send = pl.multiple_of(start + (1 - bit) * size, 8)
                copy = pltpu.make_async_remote_copy(
                    src_ref=part.at[pl.ds(send, size), lane],
                    dst_ref=rbuf.at[k, s, pl.ds(off, size), :],
                    send_sem=rs_s.at[k, s, i], recv_sem=rs_r.at[k, s, i],
                    device_id=dev, device_id_type=MESH,
                )
                down.append((copy, keep, size, off))
                start, off = keep, off + size
            up = []
            for i in reversed(range(bits)):
                _, keep, size, _ = down[i]
                region = red.at[pl.ds(keep, size), lane]
                up.append(
                    pltpu.make_async_remote_copy(
                        src_ref=region, dst_ref=region,
                        send_sem=ag_s.at[k, s, i], recv_sem=ag_r.at[k, s, i],
                        device_id=partner(order[i])[1], device_id_type=MESH,
                    )
                )
            tracks.append((s, down, up))
        return lane, k, tracks

    def unit_events(unit):
        lane, k, tracks = unit

        def rs_step(i):
            for s, down, up in tracks:
                copy, keep, size, off = down[i]
                copy.wait_recv()
                total = part[pl.ds(keep, size), lane] + rbuf[k, s, pl.ds(off, size), :]
                if i + 1 < bits:
                    part[pl.ds(keep, size), lane] = total
                    down[i + 1][0].start()
                else:
                    red[pl.ds(keep, size), lane] = total
                    up[0].start()

        def ag_step(i):
            for s, down, up in tracks:
                up[i].wait_recv()
                if i + 1 < bits:
                    up[i + 1].start()

        return [functools.partial(rs_step, i) for i in range(bits)] + [
            functools.partial(ag_step, i) for i in range(bits)
        ]

    def begin(unit):
        for s, down, up in unit[2]:
            down[0][0].start()

    def multiply(h, l):
        left = jnp.concatenate([panel[h], panel[2 + h]], axis=1)
        out = dot_t(left, a_v[l], HIGH)
        for b in range(2):
            part[(2 * b + h) * half : (2 * b + h + 1) * half, l * width : (l + 1) * width] = out[
                b * half : (b + 1) * half
            ]

    units = [[make_unit(h, l) for l in range(nbl)] for h in range(2)]

    def wave(unit_list):
        return [e for group in zip(*[unit_events(u) for u in unit_list]) for e in group]

    def run(queue, number):
        for _ in range(min(number, len(queue))):
            queue.pop(0)()

    def project(lo, hi, finished):
        m = m_v[lo:hi, :hi]
        left = jnp.concatenate([panel[i] for i in range(hi // half)], axis=1)
        q = dot_nt(left, m, HIGH)
        for l in range(nbl):
            at = slice(l * width, (l + 1) * width)
            c = dot(m, red[:hi, at], HIGH)
            c_v[l, lo:hi, :] = c
            a_v[l] = a_v[l] - dot(q, c, HIGH)
            if finished:
                outs[l].start()
                couts[l].start()

    outs = [
        pltpu.make_async_copy(a_v.at[l], rem_hbm.at[:, l, :], r_sem.at[l]) for l in range(nbl)
    ]
    couts = [
        pltpu.make_async_copy(c_v.at[l], coef_hbm.at[:, l, :], c_sem.at[l]) for l in range(nbl)
    ]

    @pl.when(first)
    def _():
        for h in range(2):
            ploads[h].wait()
            for up, side in pieces[h]:
                side.start()
        for h in range(2):
            for up, side in pieces[h]:
                up.start()
        loads[0].wait()
        for h in range(2):
            for up, side in pieces[h]:
                side.wait_recv()
            multiply(h, 0)
            begin(units[h][0])
        queue = wave([units[0][0], units[1][0]])
        for l in range(1, nbl):
            loads[l].wait()
            multiply(0, l)
            multiply(1, l)
            run(queue, 2)
        run(queue, len(queue))
        rest = [units[h][l] for h in range(2) for l in range(1, nbl)]
        for u in rest:
            begin(u)
        gram[core] = red[:, :width]
        side = pltpu.make_async_remote_copy(
            src_ref=gram.at[core], dst_ref=gram.at[core], send_sem=gss.at[0], recv_sem=gsr.at[0],
            device_id=sibling, device_id_type=MESH,
        )
        side.start()
        line = lax.broadcasted_iota(jnp.int32, (half, half), 0)
        lane = lax.broadcasted_iota(jnp.int32, (half, half), 1)
        m_v[...] = jnp.zeros_like(m_v)
        for b in range(blocks):
            at = slice(b * half, (b + 1) * half)
            m_v[at, at] = jnp.where(line == lane, 1.0, 0.0)
        side.wait_recv()
        s_v[:, :width] = gram[0]
        s_v[:, width:] = gram[1]
        queue = wave(rest)
        share = -(-len(queue) // (2 * blocks - 1))
        panels = half // PANEL
        for b in range(blocks):
            lo, hi = b * half, (b + 1) * half
            sref[:, :half] = s_v[lo:hi, lo:hi]
            sref[:, half:] = jnp.where(line == lane, 1.0, 0.0)
            factor_panels(sref, uref, half, 0, panels // 2)
            run(queue, share)
            factor_panels(sref, uref, half, panels // 2, panels)
            inv = jnp.where(line >= lane, uref[:, half:], 0.0)
            if b > 0:
                m_v[lo:hi, :lo] = full(inv, m_v[lo:hi, :lo])
            m_v[lo:hi, lo:hi] = inv
            for up, _ in mpieces[b]:
                up.start()
            if hi < n:
                u = full(inv, s_v[lo:hi, hi:])
                s_v[hi:, hi:] = s_v[hi:, hi:] - full_t(u, u)
                m_v[hi:, :hi] = m_v[hi:, :hi] - full_t(u, m_v[lo:hi, :hi])
            run(queue, share)
        run(queue, len(queue))
        project(0, width, False)
        project(width, width + half, False)
        for h in range(2):
            for up, other in pieces[h]:
                up.wait_send()
        for b in range(blocks):
            for up, _ in mpieces[b]:
                up.wait_send()
        side.wait_send()

    @pl.when(later)
    def _():
        m_v[:half, half:width] = jnp.zeros((half, half), jnp.float32)
        for p in pieces[0]:
            forward(p)
        for c in loads:
            c.wait()
        for up, side in pieces[0]:
            side.wait_recv()
        for l in range(nbl):
            multiply(0, l)
            begin(units[0][l])
        queue = wave(units[0])
        for i, p in enumerate(pieces[1]):
            forward(p)
            run(queue, nbl - 1)
        for up, side in pieces[1]:
            side.wait_recv()
        for l in range(nbl):
            multiply(1, l)
            begin(units[1][l])
            run(queue, 1)
        run(queue, len(queue))
        queue = wave(units[1])
        run(queue, nbl * bits)
        for p in mpieces[0]:
            forward(p)
        run(queue, nbl)
        for p in mpieces[1]:
            forward(p)
        run(queue, len(queue))
        for p in mpieces[2]:
            forward(p)

        @pl.when(inner)
        def _():
            for p in mpieces[3]:
                forward(p)

        for b in range(2):
            for up, side in mpieces[b]:
                side.wait_recv()
        project(0, width, False)
        for up, side in mpieces[2]:
            side.wait_recv()
        project(width, width + half, False)

        @pl.when(last)
        def _():
            for p in mpieces[3]:
                forward(p)

        for up, side in mpieces[3]:
            side.wait_recv()
        for group in mpieces:
            for up, side in group:
                side.wait_send()

        @pl.when(inner)
        def _():
            for group in pieces + mpieces:
                for up, side in group:
                    up.wait_send()

    project(width + half, n, True)
    for h in range(2):
        for up, side in pieces[h]:
            side.wait_send()
        for unit in units[h]:
            for s, down, up in unit[2]:
                for d in down:
                    d[0].wait_send()
                for c in up:
                    c.wait_send()
    for c in outs + couts:
        c.wait()


def solution(mesh):
    rows_n, cols_n = mesh.shape["row"], mesh.shape["col"]
    bits = rows_n.bit_length() - 1

    def on_device(matrix):
        count, nbl, width = matrix.shape
        half, n = width // 2, 2 * width
        units = 2 * nbl
        f32 = jnp.float32
        dma = pltpu.SemaphoreType.DMA
        anywhere = pl.BlockSpec(memory_space=pl.ANY)
        return pl.pallas_call(
            functools.partial(qr_kernel, rows_n, cols_n),
            out_shape=(
                jax.ShapeDtypeStruct((n, nbl, width), f32),
                jax.ShapeDtypeStruct((count, nbl, width), f32),
            ),
            in_specs=[anywhere],
            out_specs=(anywhere, anywhere),
            scratch_shapes=[
                pltpu.VMEM((nbl, count, width), f32),
                pltpu.VMEM((n // half, count, half), f32),
                pltpu.VMEM((n, nbl * width), f32),
                pltpu.VMEM((n, nbl * width), f32),
                pltpu.VMEM((units, 2, half, width), f32),
                pltpu.VMEM((2, n, width), f32),
                pltpu.VMEM((n, n), f32),
                pltpu.VMEM((n, n), f32),
                pltpu.VMEM((half, width), f32),
                pltpu.VMEM((half, width), f32),
                pltpu.VMEM((nbl, n, width), f32),
                dma((nbl,)),
                dma((2,)),
                dma((nbl,)),
                dma((nbl,)),
            ]
            + [dma((2 * PIECES,))] * 4
            + [dma((2 * n // half,))] * 4
            + [dma((1,))] * 2
            + [dma((units, 2, bits))] * 4,
            compiler_params=pltpu.CompilerParams(
                collective_id=0, has_side_effects=True, vmem_limit_bytes=32 * 1024 * 1024
            ),
            name="block_qr",
        )(matrix)

    return jax.shard_map(
        on_device,
        mesh=mesh,
        in_specs=(P("row", None, "col"),),
        out_specs=(P(None, None, "col"), P("row", None, "col")),
        check_vma=False,
    )
```

```python
import functools

import jax
import jax.numpy as jnp
from jax import lax
from jax.experimental import pallas as pl
from jax.experimental.pallas import tpu as pltpu
from jax.sharding import PartitionSpec as P

HIGH = lax.Precision.HIGH
MESH = pl.DeviceIdType.MESH
PIECES = 4
PANEL = 8


def dot_t(a, b, precision):
    return lax.dot_general(
        a, b, (((0,), (0,)), ((), ())), precision=precision, preferred_element_type=jnp.float32
    )


def dot(a, b, precision):
    return jnp.dot(a, b, precision=precision, preferred_element_type=jnp.float32)


def dot_nt(a, b, precision):
    return lax.dot_general(
        a, b, (((1,), (1,)), ((), ())), precision=precision, preferred_element_type=jnp.float32
    )


def split(x):
    a = x.astype(jnp.bfloat16).astype(jnp.float32)
    b = (x - a).astype(jnp.bfloat16).astype(jnp.float32)
    c = (x - a - b).astype(jnp.bfloat16).astype(jnp.float32)
    return a, b, c


def stack_left(x, axis):
    a, b, c = split(x)
    return jnp.concatenate([a, a, b, b, a, c], axis=axis).astype(jnp.bfloat16)


def stack_right(x):
    a, b, c = split(x)
    return jnp.concatenate([a, b, a, b, c, a], axis=0).astype(jnp.bfloat16)


def full_t(a, b):
    return dot_t(stack_left(a, 0), stack_right(b), None)


def full(a, b):
    return dot(stack_left(a, 1), stack_right(b), None)


def factor_panels(sref, uref, size, begin, end):
    def panel_step(p, carry):
        base = pl.multiple_of(p * PANEL, PANEL)
        rows = sref[pl.ds(base, PANEL), :]
        near = pltpu.roll(rows[:, :size], lax.rem(size - base, size), 1)
        e = {}
        for i in range(PANEL):
            for k in range(i, PANEL):
                e[i, k] = jnp.broadcast_to(near[i : i + 1, k : k + 1], (1, size))
        s = [[rows[i : i + 1, :size], rows[i : i + 1, size:]] for i in range(PANEL)]
        us = []
        for j in range(PANEL):
            d = e[j, j]
            inv = pl.reciprocal(d, approx=True)
            root = lax.rsqrt(d)
            us.append(jnp.concatenate([s[j][0] * root, s[j][1] * root], axis=1))
            if j + 1 < PANEL:
                square = e[j, j + 1] * e[j, j + 1]
                e[j + 1, j + 1] = e[j + 1, j + 1] - square * inv
            for i in range(j + 1, PANEL):
                t = e[j, i] * inv
                for k in range(i, PANEL):
                    if (i, k) != (j + 1, j + 1):
                        e[i, k] = e[i, k] - t * e[j, k]
                s[i] = [s[i][0] - t * s[j][0], s[i][1] - t * s[j][1]]
        u = jnp.concatenate(us, axis=0)
        uref[pl.ds(base, PANEL), :] = u
        sref[...] = sref[...] - full_t(u[:, :size], u)
        return carry

    lax.fori_loop(begin, end, panel_step, 0)


def qr_kernel(
    rows_n, cols_n, a_hbm, coef_hbm, rem_hbm,
    a_v, panel, part, red, rbuf, gram, s_v, m_v, sref, uref, c_v,
    load_sem, pload_sem, c_sem, r_sem,
    zs, zr, ss, sr, mzs, mzr, mss, msr, gss, gsr, rs_s, rs_r, ag_s, ag_r,
):
    row = lax.axis_index("row")
    col = lax.axis_index("col")
    chips = cols_n // 2
    bits = rows_n.bit_length() - 1
    z, core = col // 2, col % 2
    sibling = (row, col + 1 - 2 * core)
    above = (row, jnp.minimum(col + 2, cols_n - 1))
    first, last = z == 0, z == chips - 1
    later = jnp.logical_not(first)
    inner = jnp.logical_not(last)
    count, nbl, width = a_hbm.shape
    half = width // 2
    n = 2 * width
    blocks = n // half
    step = count // PIECES

    def partner(b):
        bit = (row // (1 << b)) % 2
        return bit, (row + (1 << b) * (1 - 2 * bit), col)

    loads = [
        pltpu.make_async_copy(a_hbm.at[:, l, :], a_v.at[l], load_sem.at[l]) for l in range(nbl)
    ]
    ploads = [
        pltpu.make_async_copy(
            a_hbm.at[:, 0, h * half : (h + 1) * half], panel.at[2 * core + h], pload_sem.at[h]
        )
        for h in range(2)
    ]

    @pl.when(first)
    def _():
        for c in ploads:
            c.start()

    for c in loads:
        c.start()

    barrier = pltpu.get_barrier_semaphore()
    pl.semaphore_signal(barrier, inc=1, device_id=sibling, device_id_type=MESH)
    for b in range(bits):
        pl.semaphore_signal(barrier, inc=1, device_id=partner(b)[1], device_id_type=MESH)

    @pl.when(later)
    def _():
        pl.semaphore_signal(barrier, inc=1, device_id=(row, col - 2), device_id_type=MESH)

    @pl.when(inner)
    def _():
        pl.semaphore_signal(barrier, inc=1, device_id=(row, col + 2), device_id_type=MESH)

    pl.semaphore_wait(barrier, 1 + bits + jnp.where(first, 0, 1) + jnp.where(last, 0, 1))

    def chain(ref, i, zs, zr, ss, sr):
        up = pltpu.make_async_remote_copy(
            src_ref=ref, dst_ref=ref, send_sem=zs.at[i], recv_sem=zr.at[i],
            device_id=above, device_id_type=MESH,
        )
        side = pltpu.make_async_remote_copy(
            src_ref=ref, dst_ref=ref, send_sem=ss.at[i], recv_sem=sr.at[i],
            device_id=sibling, device_id_type=MESH,
        )
        return up, side

    def forward(piece):
        up, side = piece
        up.wait_recv()

        @pl.when(inner)
        def _():
            up.start()

        side.start()

    pieces = [
        [
            chain(panel.at[2 * core + h, pl.ds(q * step, step), :], h * PIECES + q, zs, zr, ss, sr)
            for q in range(PIECES)
        ]
        for h in range(2)
    ]
    quarter = half // 4
    mpieces = [
        [
            chain(
                m_v.at[
                    pl.ds(pl.multiple_of(b * half + core * 2 * quarter + q * quarter, 8), quarter),
                    pl.ds(0, (b + 1) * half),
                ],
                2 * b + q, mzs, mzr, mss, msr,
            )
            for q in range(2)
        ]
        for b in range(blocks)
    ]

    def make_unit(h, l):
        lane = pl.ds(l * width, width)
        k = h * nbl + l
        tracks = []
        for s in range(2):
            order = [(i + s * (bits // 2)) % bits for i in range(bits)]
            start, size, off = (2 * s + h) * half, half, 0
            down = []
            for i, b in enumerate(order):
                bit, dev = partner(b)
                size //= 2
                keep = pl.multiple_of(start + bit * size, 8)
                send = pl.multiple_of(start + (1 - bit) * size, 8)
                copy = pltpu.make_async_remote_copy(
                    src_ref=part.at[pl.ds(send, size), lane],
                    dst_ref=rbuf.at[k, s, pl.ds(off, size), :],
                    send_sem=rs_s.at[k, s, i], recv_sem=rs_r.at[k, s, i],
                    device_id=dev, device_id_type=MESH,
                )
                down.append((copy, keep, size, off))
                start, off = keep, off + size
            up = []
            for i in reversed(range(bits)):
                _, keep, size, _ = down[i]
                region = red.at[pl.ds(keep, size), lane]
                up.append(
                    pltpu.make_async_remote_copy(
                        src_ref=region, dst_ref=region,
                        send_sem=ag_s.at[k, s, i], recv_sem=ag_r.at[k, s, i],
                        device_id=partner(order[i])[1], device_id_type=MESH,
                    )
                )
            tracks.append((s, down, up))
        return lane, k, tracks

    def unit_events(unit):
        lane, k, tracks = unit

        def rs_step(i):
            for s, down, up in tracks:
                copy, keep, size, off = down[i]
                copy.wait_recv()
                total = part[pl.ds(keep, size), lane] + rbuf[k, s, pl.ds(off, size), :]
                if i + 1 < bits:
                    part[pl.ds(keep, size), lane] = total
                    down[i + 1][0].start()
                else:
                    red[pl.ds(keep, size), lane] = total
                    up[0].start()

        def ag_step(i):
            for s, down, up in tracks:
                up[i].wait_recv()
                if i + 1 < bits:
                    up[i + 1].start()

        return [functools.partial(rs_step, i) for i in range(bits)] + [
            functools.partial(ag_step, i) for i in range(bits)
        ]

    def begin(unit):
        for s, down, up in unit[2]:
            down[0][0].start()

    def multiply(h, l):
        left = jnp.concatenate([panel[h], panel[2 + h]], axis=1)
        out = dot_t(left, a_v[l], HIGH)
        for b in range(2):
            part[(2 * b + h) * half : (2 * b + h + 1) * half, l * width : (l + 1) * width] = out[
                b * half : (b + 1) * half
            ]

    units = [[make_unit(h, l) for l in range(nbl)] for h in range(2)]

    def wave(unit_list):
        return [e for group in zip(*[unit_events(u) for u in unit_list]) for e in group]

    def run(queue, number):
        for _ in range(min(number, len(queue))):
            queue.pop(0)()

    def project(lo, hi, finished):
        m = m_v[lo:hi, :hi]
        left = jnp.concatenate([panel[i] for i in range(hi // half)], axis=1)
        q = dot_nt(left, m, HIGH)
        for l in range(nbl):
            at = slice(l * width, (l + 1) * width)
            c = dot(m, red[:hi, at], HIGH)
            c_v[l, lo:hi, :] = c
            couts[lo, l].start()
            a_v[l] = a_v[l] - dot(q, c, HIGH)
            if finished:
                outs[l].start()

    outs = [
        pltpu.make_async_copy(a_v.at[l], rem_hbm.at[:, l, :], r_sem.at[l]) for l in range(nbl)
    ]
    groups = [(0, width), (width, width + half), (width + half, n)]
    couts = {
        (lo, l): pltpu.make_async_copy(
            c_v.at[l, lo:hi, :], coef_hbm.at[lo:hi, l, :], c_sem.at[g * nbl + l]
        )
        for g, (lo, hi) in enumerate(groups)
        for l in range(nbl)
    }

    @pl.when(first)
    def _():
        for h in range(2):
            ploads[h].wait()
            for up, side in pieces[h]:
                side.start()
        for h in range(2):
            for up, side in pieces[h]:
                up.start()
        loads[0].wait()
        for h in range(2):
            for up, side in pieces[h]:
                side.wait_recv()
            multiply(h, 0)
            begin(units[h][0])
        queue = wave([units[0][0], units[1][0]])
        for l in range(1, nbl):
            loads[l].wait()
            multiply(0, l)
            multiply(1, l)
            run(queue, 2)
        run(queue, len(queue))
        rest = [units[h][l] for h in range(2) for l in range(1, nbl)]
        for u in rest:
            begin(u)
        gram[core] = red[:, :width]
        side = pltpu.make_async_remote_copy(
            src_ref=gram.at[core], dst_ref=gram.at[core], send_sem=gss.at[0], recv_sem=gsr.at[0],
            device_id=sibling, device_id_type=MESH,
        )
        side.start()
        line = lax.broadcasted_iota(jnp.int32, (half, half), 0)
        lane = lax.broadcasted_iota(jnp.int32, (half, half), 1)
        m_v[...] = jnp.zeros_like(m_v)
        for b in range(blocks):
            at = slice(b * half, (b + 1) * half)
            m_v[at, at] = jnp.where(line == lane, 1.0, 0.0)
        side.wait_recv()
        s_v[:, :width] = gram[0]
        s_v[:, width:] = gram[1]
        queue = wave(rest)
        share = -(-len(queue) // (2 * blocks - 1))
        panels = half // PANEL
        for b in range(blocks):
            lo, hi = b * half, (b + 1) * half
            sref[:, :half] = s_v[lo:hi, lo:hi]
            sref[:, half:] = jnp.where(line == lane, 1.0, 0.0)
            factor_panels(sref, uref, half, 0, panels // 2)
            run(queue, share)
            factor_panels(sref, uref, half, panels // 2, panels)
            inv = jnp.where(line >= lane, uref[:, half:], 0.0)
            if b > 0:
                m_v[lo:hi, :lo] = full(inv, m_v[lo:hi, :lo])
            m_v[lo:hi, lo:hi] = inv
            for up, _ in mpieces[b]:
                up.start()
            if hi < n:
                u = full(inv, s_v[lo:hi, hi:])
                s_v[hi:, hi:] = s_v[hi:, hi:] - full_t(u, u)
                m_v[hi:, :hi] = m_v[hi:, :hi] - full_t(u, m_v[lo:hi, :hi])
            run(queue, share)
        run(queue, len(queue))
        project(0, width, False)
        project(width, width + half, False)
        for h in range(2):
            for up, other in pieces[h]:
                up.wait_send()
        for b in range(blocks):
            for up, _ in mpieces[b]:
                up.wait_send()
        side.wait_send()

    @pl.when(later)
    def _():
        m_v[:half, half:width] = jnp.zeros((half, half), jnp.float32)
        for p in pieces[0]:
            forward(p)
        for c in loads:
            c.wait()
        for up, side in pieces[0]:
            side.wait_recv()
        for l in range(nbl):
            multiply(0, l)
            begin(units[0][l])
        queue = wave(units[0])
        for i, p in enumerate(pieces[1]):
            forward(p)
            run(queue, nbl - 1)
        for up, side in pieces[1]:
            side.wait_recv()
        for l in range(nbl):
            multiply(1, l)
            begin(units[1][l])
            run(queue, 1)
        run(queue, len(queue))
        queue = wave(units[1])
        run(queue, nbl * bits)
        for p in mpieces[0]:
            forward(p)
        run(queue, nbl)
        for p in mpieces[1]:
            forward(p)
        run(queue, len(queue))
        for p in mpieces[2]:
            forward(p)

        @pl.when(inner)
        def _():
            for p in mpieces[3]:
                forward(p)

        for b in range(2):
            for up, side in mpieces[b]:
                side.wait_recv()
        project(0, width, False)
        for up, side in mpieces[2]:
            side.wait_recv()
        project(width, width + half, False)

        @pl.when(last)
        def _():
            for p in mpieces[3]:
                forward(p)

        for up, side in mpieces[3]:
            side.wait_recv()
        for group in mpieces:
            for up, side in group:
                side.wait_send()

        @pl.when(inner)
        def _():
            for group in pieces + mpieces:
                for up, side in group:
                    up.wait_send()

    project(width + half, n, True)
    for h in range(2):
        for up, side in pieces[h]:
            side.wait_send()
        for unit in units[h]:
            for s, down, up in unit[2]:
                for d in down:
                    d[0].wait_send()
                for c in up:
                    c.wait_send()
    for c in outs + list(couts.values()):
        c.wait()


def solution(mesh):
    rows_n, cols_n = mesh.shape["row"], mesh.shape["col"]
    bits = rows_n.bit_length() - 1

    def on_device(matrix):
        count, nbl, width = matrix.shape
        half, n = width // 2, 2 * width
        units = 2 * nbl
        f32 = jnp.float32
        dma = pltpu.SemaphoreType.DMA
        anywhere = pl.BlockSpec(memory_space=pl.ANY)
        return pl.pallas_call(
            functools.partial(qr_kernel, rows_n, cols_n),
            out_shape=(
                jax.ShapeDtypeStruct((n, nbl, width), f32),
                jax.ShapeDtypeStruct((count, nbl, width), f32),
            ),
            in_specs=[anywhere],
            out_specs=(anywhere, anywhere),
            scratch_shapes=[
                pltpu.VMEM((nbl, count, width), f32),
                pltpu.VMEM((n // half, count, half), f32),
                pltpu.VMEM((n, nbl * width), f32),
                pltpu.VMEM((n, nbl * width), f32),
                pltpu.VMEM((units, 2, half, width), f32),
                pltpu.VMEM((2, n, width), f32),
                pltpu.VMEM((n, n), f32),
                pltpu.VMEM((n, n), f32),
                pltpu.VMEM((half, width), f32),
                pltpu.VMEM((half, width), f32),
                pltpu.VMEM((nbl, n, width), f32),
                dma((nbl,)),
                dma((2,)),
                dma((3 * nbl,)),
                dma((nbl,)),
            ]
            + [dma((2 * PIECES,))] * 4
            + [dma((2 * n // half,))] * 4
            + [dma((1,))] * 2
            + [dma((units, 2, bits))] * 4,
            compiler_params=pltpu.CompilerParams(
                collective_id=0, has_side_effects=True, vmem_limit_bytes=48 * 1024 * 1024
            ),
            name="block_qr",
        )(matrix)

    return jax.shard_map(
        on_device,
        mesh=mesh,
        in_specs=(P("row", None, "col"),),
        out_specs=(P(None, None, "col"), P("row", None, "col")),
        check_vma=False,
    )
```

```python
import functools

import jax
import jax.numpy as jnp
from jax import lax
from jax.experimental import pallas as pl
from jax.experimental.pallas import tpu as pltpu
from jax.sharding import PartitionSpec as P

HIGH = lax.Precision.HIGH
MESH = pl.DeviceIdType.MESH
PIECES = 4
PANEL = 8


def dot_t(a, b, precision):
    return lax.dot_general(
        a, b, (((0,), (0,)), ((), ())), precision=precision, preferred_element_type=jnp.float32
    )


def dot(a, b, precision):
    return jnp.dot(a, b, precision=precision, preferred_element_type=jnp.float32)


def dot_nt(a, b, precision):
    return lax.dot_general(
        a, b, (((1,), (1,)), ((), ())), precision=precision, preferred_element_type=jnp.float32
    )


def split(x):
    a = x.astype(jnp.bfloat16).astype(jnp.float32)
    b = (x - a).astype(jnp.bfloat16).astype(jnp.float32)
    c = (x - a - b).astype(jnp.bfloat16).astype(jnp.float32)
    return a, b, c


def stack_left(x, axis):
    a, b, c = split(x)
    return jnp.concatenate([a, a, b, b, a, c], axis=axis).astype(jnp.bfloat16)


def stack_right(x):
    a, b, c = split(x)
    return jnp.concatenate([a, b, a, b, c, a], axis=0).astype(jnp.bfloat16)


def full_t(a, b):
    return dot_t(stack_left(a, 0), stack_right(b), None)


def full(a, b):
    return dot(stack_left(a, 1), stack_right(b), None)


def factor_panels(sref, uref, size, begin, end):
    def panel_step(p, carry):
        base = pl.multiple_of(p * PANEL, PANEL)
        rows = sref[pl.ds(base, PANEL), :]
        near = pltpu.roll(rows[:, :size], lax.rem(size - base, size), 1)
        e = {}
        for i in range(PANEL):
            for k in range(i, PANEL):
                e[i, k] = jnp.broadcast_to(near[i : i + 1, k : k + 1], (1, size))
        s = [[rows[i : i + 1, :size], rows[i : i + 1, size:]] for i in range(PANEL)]
        us = []
        for j in range(PANEL):
            d = e[j, j]
            inv = pl.reciprocal(d, approx=True)
            root = lax.rsqrt(d)
            us.append(jnp.concatenate([s[j][0] * root, s[j][1] * root], axis=1))
            if j + 1 < PANEL:
                square = e[j, j + 1] * e[j, j + 1]
                e[j + 1, j + 1] = e[j + 1, j + 1] - square * inv
            for i in range(j + 1, PANEL):
                t = e[j, i] * inv
                for k in range(i, PANEL):
                    if (i, k) != (j + 1, j + 1):
                        e[i, k] = e[i, k] - t * e[j, k]
                s[i] = [s[i][0] - t * s[j][0], s[i][1] - t * s[j][1]]
        u = jnp.concatenate(us, axis=0)
        uref[pl.ds(base, PANEL), :] = u
        sref[...] = sref[...] - full_t(u[:, :size], u)
        return carry

    lax.fori_loop(begin, end, panel_step, 0)


def qr_kernel(
    rows_n, cols_n, a_hbm, coef_hbm, rem_hbm,
    a_v, panel, part, red, rbuf, gram, s_v, m_v, sref, uref, c_v,
    load_sem, pload_sem, c_sem, r_sem,
    zs, zr, ss, sr, mzs, mzr, mss, msr, gss, gsr, rs_s, rs_r, ag_s, ag_r,
):
    row = lax.axis_index("row")
    col = lax.axis_index("col")
    chips = cols_n // 2
    bits = rows_n.bit_length() - 1
    z, core = col // 2, col % 2
    sibling = (row, col + 1 - 2 * core)
    above = (row, jnp.minimum(col + 2, cols_n - 1))
    first, last = z == 0, z == chips - 1
    later = jnp.logical_not(first)
    inner = jnp.logical_not(last)
    count, nbl, width = a_hbm.shape
    half = width // 2
    n = 2 * width
    blocks = n // half
    step = count // PIECES

    def partner(b):
        bit = (row // (1 << b)) % 2
        return bit, (row + (1 << b) * (1 - 2 * bit), col)

    loads = [
        pltpu.make_async_copy(a_hbm.at[:, l, :], a_v.at[l], load_sem.at[l]) for l in range(nbl)
    ]
    ploads = [
        pltpu.make_async_copy(
            a_hbm.at[:, 0, h * half : (h + 1) * half], panel.at[2 * core + h], pload_sem.at[h]
        )
        for h in range(2)
    ]

    @pl.when(first)
    def _():
        for c in ploads:
            c.start()

    for c in loads:
        c.start()

    barrier = pltpu.get_barrier_semaphore()
    pl.semaphore_signal(barrier, inc=1, device_id=sibling, device_id_type=MESH)
    for b in range(bits):
        pl.semaphore_signal(barrier, inc=1, device_id=partner(b)[1], device_id_type=MESH)

    @pl.when(later)
    def _():
        pl.semaphore_signal(barrier, inc=1, device_id=(row, col - 2), device_id_type=MESH)

    @pl.when(inner)
    def _():
        pl.semaphore_signal(barrier, inc=1, device_id=(row, col + 2), device_id_type=MESH)

    pl.semaphore_wait(barrier, 1 + bits + jnp.where(first, 0, 1) + jnp.where(last, 0, 1))

    def chain(ref, i, zs, zr, ss, sr):
        up = pltpu.make_async_remote_copy(
            src_ref=ref, dst_ref=ref, send_sem=zs.at[i], recv_sem=zr.at[i],
            device_id=above, device_id_type=MESH,
        )
        side = pltpu.make_async_remote_copy(
            src_ref=ref, dst_ref=ref, send_sem=ss.at[i], recv_sem=sr.at[i],
            device_id=sibling, device_id_type=MESH,
        )
        return up, side

    def forward(piece):
        up, side = piece
        up.wait_recv()

        @pl.when(inner)
        def _():
            up.start()

        side.start()

    pieces = [
        [
            chain(panel.at[2 * core + h, pl.ds(q * step, step), :], h * PIECES + q, zs, zr, ss, sr)
            for q in range(PIECES)
        ]
        for h in range(2)
    ]
    quarter = half // 4
    mpieces = [
        [
            chain(
                m_v.at[
                    pl.ds(pl.multiple_of(b * half + core * 2 * quarter + q * quarter, 8), quarter),
                    pl.ds(0, (b + 1) * half),
                ],
                2 * b + q, mzs, mzr, mss, msr,
            )
            for q in range(2)
        ]
        for b in range(blocks)
    ]

    def make_unit(h, l):
        lane = pl.ds(l * width, width)
        k = h * nbl + l
        tracks = []
        for s in range(2):
            order = [(i + s * (bits // 2)) % bits for i in range(bits)]
            start, size, off = (2 * s + h) * half, half, 0
            down = []
            for i, b in enumerate(order):
                bit, dev = partner(b)
                size //= 2
                keep = pl.multiple_of(start + bit * size, 8)
                send = pl.multiple_of(start + (1 - bit) * size, 8)
                copy = pltpu.make_async_remote_copy(
                    src_ref=part.at[pl.ds(send, size), lane],
                    dst_ref=rbuf.at[k, s, pl.ds(off, size), :],
                    send_sem=rs_s.at[k, s, i], recv_sem=rs_r.at[k, s, i],
                    device_id=dev, device_id_type=MESH,
                )
                down.append((copy, keep, size, off))
                start, off = keep, off + size
            up = []
            for i in reversed(range(bits)):
                _, keep, size, _ = down[i]
                region = red.at[pl.ds(keep, size), lane]
                up.append(
                    pltpu.make_async_remote_copy(
                        src_ref=region, dst_ref=region,
                        send_sem=ag_s.at[k, s, i], recv_sem=ag_r.at[k, s, i],
                        device_id=partner(order[i])[1], device_id_type=MESH,
                    )
                )
            tracks.append((s, down, up))
        return lane, k, tracks

    def unit_events(unit):
        lane, k, tracks = unit

        def rs_step(i):
            for s, down, up in tracks:
                copy, keep, size, off = down[i]
                copy.wait_recv()
                total = part[pl.ds(keep, size), lane] + rbuf[k, s, pl.ds(off, size), :]
                if i + 1 < bits:
                    part[pl.ds(keep, size), lane] = total
                    down[i + 1][0].start()
                else:
                    red[pl.ds(keep, size), lane] = total
                    up[0].start()

        def ag_step(i):
            for s, down, up in tracks:
                up[i].wait_recv()
                if i + 1 < bits:
                    up[i + 1].start()

        return [functools.partial(rs_step, i) for i in range(bits)] + [
            functools.partial(ag_step, i) for i in range(bits)
        ]

    def begin(unit):
        for s, down, up in unit[2]:
            down[0][0].start()

    def multiply(h, l):
        left = jnp.concatenate([panel[h], panel[2 + h]], axis=1)
        out = dot_t(left, a_v[l], HIGH)
        for b in range(2):
            part[(2 * b + h) * half : (2 * b + h + 1) * half, l * width : (l + 1) * width] = out[
                b * half : (b + 1) * half
            ]

    units = [[make_unit(h, l) for l in range(nbl)] for h in range(2)]

    def wave(unit_list):
        return [e for group in zip(*[unit_events(u) for u in unit_list]) for e in group]

    def run(queue, number):
        for _ in range(min(number, len(queue))):
            queue.pop(0)()

    def project(lo, hi, finished):
        m = m_v[lo:hi, :hi]
        left = jnp.concatenate([panel[i] for i in range(hi // half)], axis=1)
        q = dot_nt(left, m, HIGH)
        for l in range(nbl):
            at = slice(l * width, (l + 1) * width)
            c = dot(m, red[:hi, at], HIGH)
            c_v[l, lo:hi, :] = c
            couts[lo, l].start()
            a_v[l] = a_v[l] - dot(q, c, HIGH)
            if finished:
                outs[l].start()

    outs = [
        pltpu.make_async_copy(a_v.at[l], rem_hbm.at[:, l, :], r_sem.at[l]) for l in range(nbl)
    ]
    groups = [(0, width), (width, width + half), (width + half, n)]
    couts = {
        (lo, l): pltpu.make_async_copy(
            c_v.at[l, lo:hi, :], coef_hbm.at[lo:hi, l, :], c_sem.at[g * nbl + l]
        )
        for g, (lo, hi) in enumerate(groups)
        for l in range(nbl)
    }

    @pl.when(first)
    def _():
        for h in range(2):
            ploads[h].wait()
            for up, side in pieces[h]:
                side.start()
        for h in range(2):
            for up, side in pieces[h]:
                up.start()
        loads[0].wait()
        for h in range(2):
            for up, side in pieces[h]:
                side.wait_recv()
            multiply(h, 0)
            begin(units[h][0])
        queue = wave([units[0][0], units[1][0]])
        rest = [units[h][l] for l in range(1, nbl) for h in range(2)]
        for l in range(1, nbl):
            loads[l].wait()
            multiply(0, l)
            multiply(1, l)
            run(queue, 2)
            for h in range(2):
                begin(units[h][l])
        run(queue, len(queue))
        gram[core] = red[:, :width]
        side = pltpu.make_async_remote_copy(
            src_ref=gram.at[core], dst_ref=gram.at[core], send_sem=gss.at[0], recv_sem=gsr.at[0],
            device_id=sibling, device_id_type=MESH,
        )
        side.start()
        line = lax.broadcasted_iota(jnp.int32, (half, half), 0)
        lane = lax.broadcasted_iota(jnp.int32, (half, half), 1)
        m_v[...] = jnp.zeros_like(m_v)
        for b in range(blocks):
            at = slice(b * half, (b + 1) * half)
            m_v[at, at] = jnp.where(line == lane, 1.0, 0.0)
        side.wait_recv()
        s_v[:, :width] = gram[0]
        s_v[:, width:] = gram[1]
        queue = wave(rest)
        share = -(-len(queue) // (2 * blocks - 1))
        panels = half // PANEL
        for b in range(blocks):
            lo, hi = b * half, (b + 1) * half
            sref[:, :half] = s_v[lo:hi, lo:hi]
            sref[:, half:] = jnp.where(line == lane, 1.0, 0.0)
            factor_panels(sref, uref, half, 0, panels // 2)
            run(queue, share)
            factor_panels(sref, uref, half, panels // 2, panels)
            inv = jnp.where(line >= lane, uref[:, half:], 0.0)
            if b > 0:
                m_v[lo:hi, :lo] = full(inv, m_v[lo:hi, :lo])
            m_v[lo:hi, lo:hi] = inv
            for up, _ in mpieces[b]:
                up.start()
            if hi < n:
                u = full(inv, s_v[lo:hi, hi:])
                s_v[hi:, hi:] = s_v[hi:, hi:] - full_t(u, u)
                m_v[hi:, :hi] = m_v[hi:, :hi] - full_t(u, m_v[lo:hi, :hi])
            run(queue, share)
        run(queue, len(queue))
        project(0, width, False)
        project(width, width + half, False)
        for h in range(2):
            for up, other in pieces[h]:
                up.wait_send()
        for b in range(blocks):
            for up, _ in mpieces[b]:
                up.wait_send()
        side.wait_send()

    @pl.when(later)
    def _():
        m_v[:half, half:width] = jnp.zeros((half, half), jnp.float32)
        for p in pieces[0]:
            forward(p)
        for c in loads:
            c.wait()
        for up, side in pieces[0]:
            side.wait_recv()
        for l in range(nbl):
            multiply(0, l)
            begin(units[0][l])
        queue = wave(units[0])
        for i, p in enumerate(pieces[1]):
            forward(p)
            run(queue, nbl - 1)
        for up, side in pieces[1]:
            side.wait_recv()
        for l in range(nbl):
            multiply(1, l)
            begin(units[1][l])
            run(queue, 1)
        run(queue, len(queue))
        queue = wave(units[1])
        run(queue, nbl * bits)
        for p in mpieces[0]:
            forward(p)
        run(queue, nbl)
        for p in mpieces[1]:
            forward(p)
        run(queue, len(queue))
        @pl.when(inner)
        def _():
            for p in mpieces[2] + mpieces[3]:
                forward(p)

        for b in range(2):
            for up, side in mpieces[b]:
                side.wait_recv()
        project(0, width, False)

        @pl.when(last)
        def _():
            for p in mpieces[2]:
                forward(p)

        for up, side in mpieces[2]:
            side.wait_recv()
        project(width, width + half, False)

        @pl.when(last)
        def _():
            for p in mpieces[3]:
                forward(p)

        for up, side in mpieces[3]:
            side.wait_recv()
        for group in mpieces:
            for up, side in group:
                side.wait_send()

        @pl.when(inner)
        def _():
            for group in pieces + mpieces:
                for up, side in group:
                    up.wait_send()

    project(width + half, n, True)
    for h in range(2):
        for up, side in pieces[h]:
            side.wait_send()
        for unit in units[h]:
            for s, down, up in unit[2]:
                for d in down:
                    d[0].wait_send()
                for c in up:
                    c.wait_send()
    for c in outs + list(couts.values()):
        c.wait()


def solution(mesh):
    rows_n, cols_n = mesh.shape["row"], mesh.shape["col"]
    bits = rows_n.bit_length() - 1

    def on_device(matrix):
        count, nbl, width = matrix.shape
        half, n = width // 2, 2 * width
        units = 2 * nbl
        f32 = jnp.float32
        dma = pltpu.SemaphoreType.DMA
        anywhere = pl.BlockSpec(memory_space=pl.ANY)
        return pl.pallas_call(
            functools.partial(qr_kernel, rows_n, cols_n),
            out_shape=(
                jax.ShapeDtypeStruct((n, nbl, width), f32),
                jax.ShapeDtypeStruct((count, nbl, width), f32),
            ),
            in_specs=[anywhere],
            out_specs=(anywhere, anywhere),
            scratch_shapes=[
                pltpu.VMEM((nbl, count, width), f32),
                pltpu.VMEM((n // half, count, half), f32),
                pltpu.VMEM((n, nbl * width), f32),
                pltpu.VMEM((n, nbl * width), f32),
                pltpu.VMEM((units, 2, half, width), f32),
                pltpu.VMEM((2, n, width), f32),
                pltpu.VMEM((n, n), f32),
                pltpu.VMEM((n, n), f32),
                pltpu.VMEM((half, width), f32),
                pltpu.VMEM((half, width), f32),
                pltpu.VMEM((nbl, n, width), f32),
                dma((nbl,)),
                dma((2,)),
                dma((3 * nbl,)),
                dma((nbl,)),
            ]
            + [dma((2 * PIECES,))] * 4
            + [dma((2 * n // half,))] * 4
            + [dma((1,))] * 2
            + [dma((units, 2, bits))] * 4,
            compiler_params=pltpu.CompilerParams(
                collective_id=0, has_side_effects=True, vmem_limit_bytes=48 * 1024 * 1024
            ),
            name="block_qr",
        )(matrix)

    return jax.shard_map(
        on_device,
        mesh=mesh,
        in_specs=(P("row", None, "col"),),
        out_specs=(P(None, None, "col"), P("row", None, "col")),
        check_vma=False,
    )
```

```python
import functools

import jax
import jax.numpy as jnp
from jax import lax
from jax.experimental import pallas as pl
from jax.experimental.pallas import tpu as pltpu
from jax.sharding import PartitionSpec as P

HIGH = lax.Precision.HIGH
HIGHEST = lax.Precision.HIGHEST
MESH = pl.DeviceIdType.MESH
PIECES = 4
PANEL = 16


def dot_t(a, b, precision):
    return lax.dot_general(
        a, b, (((0,), (0,)), ((), ())), precision=precision, preferred_element_type=jnp.float32
    )


def dot(a, b, precision):
    return jnp.dot(a, b, precision=precision, preferred_element_type=jnp.float32)


def dot_nt(a, b, precision):
    return lax.dot_general(
        a, b, (((1,), (1,)), ((), ())), precision=precision, preferred_element_type=jnp.float32
    )


def factor_panels(sref, uref, size, begin, end):
    def panel_step(p, carry):
        base = pl.multiple_of(p * PANEL, PANEL)
        rows = sref[pl.ds(base, PANEL), :]
        near = pltpu.roll(rows[:, :size], lax.rem(size - base, size), 1)
        e = {}
        for i in range(PANEL):
            for k in range(i, PANEL):
                e[i, k] = jnp.broadcast_to(near[i : i + 1, k : k + 1], (1, size))
        s = [[rows[i : i + 1, :size], rows[i : i + 1, size:]] for i in range(PANEL)]
        us = []
        for j in range(PANEL):
            d = e[j, j]
            inv = pl.reciprocal(d, approx=True)
            root = lax.rsqrt(d)
            us.append(jnp.concatenate([s[j][0] * root, s[j][1] * root], axis=1))
            if j + 1 < PANEL:
                square = e[j, j + 1] * e[j, j + 1]
                e[j + 1, j + 1] = e[j + 1, j + 1] - square * inv
            for i in range(j + 1, PANEL):
                t = e[j, i] * inv
                for k in range(i, PANEL):
                    if (i, k) != (j + 1, j + 1):
                        e[i, k] = e[i, k] - t * e[j, k]
                s[i] = [s[i][0] - t * s[j][0], s[i][1] - t * s[j][1]]
        u = jnp.concatenate(us, axis=0)
        uref[pl.ds(base, PANEL), :] = u
        sref[...] = sref[...] - dot_t(u[:, :size], u, HIGHEST)
        return carry

    lax.fori_loop(begin, end, panel_step, 0)


def qr_kernel(
    rows_n, cols_n, a_hbm, coef_hbm, rem_hbm,
    a_v, panel, part, red, rbuf, gram, s_v, m_v, sref, uref, c_v,
    load_sem, pload_sem, c_sem, r_sem,
    zs, zr, ss, sr, mzs, mzr, mss, msr, gss, gsr, rs_s, rs_r, ag_s, ag_r,
):
    row = lax.axis_index("row")
    col = lax.axis_index("col")
    chips = cols_n // 2
    bits = rows_n.bit_length() - 1
    z, core = col // 2, col % 2
    sibling = (row, col + 1 - 2 * core)
    above = (row, jnp.minimum(col + 2, cols_n - 1))
    first, last = z == 0, z == chips - 1
    later = jnp.logical_not(first)
    inner = jnp.logical_not(last)
    count, nbl, width = a_hbm.shape
    half = width // 2
    n = 2 * width
    blocks = n // half
    step = count // PIECES

    def partner(b):
        bit = (row // (1 << b)) % 2
        return bit, (row + (1 << b) * (1 - 2 * bit), col)

    loads = [
        pltpu.make_async_copy(a_hbm.at[:, l, :], a_v.at[l], load_sem.at[l]) for l in range(nbl)
    ]
    ploads = [
        pltpu.make_async_copy(
            a_hbm.at[:, 0, h * half : (h + 1) * half], panel.at[2 * core + h], pload_sem.at[h]
        )
        for h in range(2)
    ]

    @pl.when(first)
    def _():
        for c in ploads:
            c.start()

    for c in loads:
        c.start()

    barrier = pltpu.get_barrier_semaphore()
    pl.semaphore_signal(barrier, inc=1, device_id=sibling, device_id_type=MESH)
    for b in range(bits):
        pl.semaphore_signal(barrier, inc=1, device_id=partner(b)[1], device_id_type=MESH)

    @pl.when(later)
    def _():
        pl.semaphore_signal(barrier, inc=1, device_id=(row, col - 2), device_id_type=MESH)

    @pl.when(inner)
    def _():
        pl.semaphore_signal(barrier, inc=1, device_id=(row, col + 2), device_id_type=MESH)

    pl.semaphore_wait(barrier, 1 + bits + jnp.where(first, 0, 1) + jnp.where(last, 0, 1))

    def chain(ref, i, zs, zr, ss, sr):
        up = pltpu.make_async_remote_copy(
            src_ref=ref, dst_ref=ref, send_sem=zs.at[i], recv_sem=zr.at[i],
            device_id=above, device_id_type=MESH,
        )
        side = pltpu.make_async_remote_copy(
            src_ref=ref, dst_ref=ref, send_sem=ss.at[i], recv_sem=sr.at[i],
            device_id=sibling, device_id_type=MESH,
        )
        return up, side

    def forward(piece):
        up, side = piece
        up.wait_recv()

        @pl.when(inner)
        def _():
            up.start()

        side.start()

    pieces = [
        [
            chain(panel.at[2 * core + h, pl.ds(q * step, step), :], h * PIECES + q, zs, zr, ss, sr)
            for q in range(PIECES)
        ]
        for h in range(2)
    ]
    quarter = half // 4
    mpieces = [
        [
            chain(
                m_v.at[
                    pl.ds(pl.multiple_of(b * half + core * 2 * quarter + q * quarter, 8), quarter),
                    pl.ds(0, (b + 1) * half),
                ],
                2 * b + q, mzs, mzr, mss, msr,
            )
            for q in range(2)
        ]
        for b in range(blocks)
    ]

    def make_unit(h, l):
        lane = pl.ds(l * width, width)
        k = h * nbl + l
        tracks = []
        for s in range(2):
            order = [(i + s * (bits // 2)) % bits for i in range(bits)]
            start, size, off = (2 * s + h) * half, half, 0
            down = []
            for i, b in enumerate(order):
                bit, dev = partner(b)
                size //= 2
                keep = pl.multiple_of(start + bit * size, 8)
                send = pl.multiple_of(start + (1 - bit) * size, 8)
                copy = pltpu.make_async_remote_copy(
                    src_ref=part.at[pl.ds(send, size), lane],
                    dst_ref=rbuf.at[k, s, pl.ds(off, size), :],
                    send_sem=rs_s.at[k, s, i], recv_sem=rs_r.at[k, s, i],
                    device_id=dev, device_id_type=MESH,
                )
                down.append((copy, keep, size, off))
                start, off = keep, off + size
            up = []
            for i in reversed(range(bits)):
                _, keep, size, _ = down[i]
                region = red.at[pl.ds(keep, size), lane]
                up.append(
                    pltpu.make_async_remote_copy(
                        src_ref=region, dst_ref=region,
                        send_sem=ag_s.at[k, s, i], recv_sem=ag_r.at[k, s, i],
                        device_id=partner(order[i])[1], device_id_type=MESH,
                    )
                )
            tracks.append((s, down, up))
        return lane, k, tracks

    def unit_events(unit):
        lane, k, tracks = unit

        def rs_step(i):
            for s, down, up in tracks:
                copy, keep, size, off = down[i]
                copy.wait_recv()
                total = part[pl.ds(keep, size), lane] + rbuf[k, s, pl.ds(off, size), :]
                if i + 1 < bits:
                    part[pl.ds(keep, size), lane] = total
                    down[i + 1][0].start()
                else:
                    red[pl.ds(keep, size), lane] = total
                    up[0].start()

        def ag_step(i):
            for s, down, up in tracks:
                up[i].wait_recv()
                if i + 1 < bits:
                    up[i + 1].start()

        return [functools.partial(rs_step, i) for i in range(bits)] + [
            functools.partial(ag_step, i) for i in range(bits)
        ]

    def begin(unit):
        for s, down, up in unit[2]:
            down[0][0].start()

    def multiply(h, l):
        left = jnp.concatenate([panel[h], panel[2 + h]], axis=1)
        out = dot_t(left, a_v[l], HIGH)
        for b in range(2):
            part[(2 * b + h) * half : (2 * b + h + 1) * half, l * width : (l + 1) * width] = out[
                b * half : (b + 1) * half
            ]

    units = [[make_unit(h, l) for l in range(nbl)] for h in range(2)]

    def wave(unit_list):
        return [e for group in zip(*[unit_events(u) for u in unit_list]) for e in group]

    def run(queue, number):
        for _ in range(min(number, len(queue))):
            queue.pop(0)()

    def project(lo, hi, finished):
        m = m_v[lo:hi, :hi]
        left = jnp.concatenate([panel[i] for i in range(hi // half)], axis=1)
        q = dot_nt(left, m, HIGH)
        for l in range(nbl):
            at = slice(l * width, (l + 1) * width)
            c = dot(m, red[:hi, at], HIGH)
            c_v[l, lo:hi, :] = c
            couts[lo, l].start()
            a_v[l] = a_v[l] - dot(q, c, HIGH)
            if finished:
                outs[l].start()

    outs = [
        pltpu.make_async_copy(a_v.at[l], rem_hbm.at[:, l, :], r_sem.at[l]) for l in range(nbl)
    ]
    groups = [(0, width), (width, width + half), (width + half, n)]
    couts = {
        (lo, l): pltpu.make_async_copy(
            c_v.at[l, lo:hi, :], coef_hbm.at[lo:hi, l, :], c_sem.at[g * nbl + l]
        )
        for g, (lo, hi) in enumerate(groups)
        for l in range(nbl)
    }

    @pl.when(first)
    def _():
        for h in range(2):
            ploads[h].wait()
            for up, side in pieces[h]:
                side.start()
        for h in range(2):
            for up, side in pieces[h]:
                up.start()
        loads[0].wait()
        for h in range(2):
            for up, side in pieces[h]:
                side.wait_recv()
            multiply(h, 0)
            begin(units[h][0])
        queue = wave([units[0][0], units[1][0]])
        for l in range(1, nbl):
            loads[l].wait()
            multiply(0, l)
            multiply(1, l)
            run(queue, 2)
        run(queue, len(queue))
        rest = [units[h][l] for h in range(2) for l in range(1, nbl)]
        for u in rest:
            begin(u)
        gram[core] = red[:, :width]
        side = pltpu.make_async_remote_copy(
            src_ref=gram.at[core], dst_ref=gram.at[core], send_sem=gss.at[0], recv_sem=gsr.at[0],
            device_id=sibling, device_id_type=MESH,
        )
        side.start()
        line = lax.broadcasted_iota(jnp.int32, (half, half), 0)
        lane = lax.broadcasted_iota(jnp.int32, (half, half), 1)
        m_v[...] = jnp.zeros_like(m_v)
        for b in range(blocks):
            at = slice(b * half, (b + 1) * half)
            m_v[at, at] = jnp.where(line == lane, 1.0, 0.0)
        side.wait_recv()
        s_v[:, :width] = gram[0]
        s_v[:, width:] = gram[1]
        queue = wave(rest)
        share = -(-len(queue) // (2 * blocks - 1))
        panels = half // PANEL
        for b in range(blocks):
            lo, hi = b * half, (b + 1) * half
            sref[:, :half] = s_v[lo:hi, lo:hi]
            sref[:, half:] = jnp.where(line == lane, 1.0, 0.0)
            factor_panels(sref, uref, half, 0, panels // 2)
            run(queue, share)
            factor_panels(sref, uref, half, panels // 2, panels)
            inv = jnp.where(line >= lane, uref[:, half:], 0.0)
            if b > 0:
                m_v[lo:hi, :lo] = dot(inv, m_v[lo:hi, :lo], HIGHEST)
            m_v[lo:hi, lo:hi] = inv
            for up, _ in mpieces[b]:
                up.start()
            if hi < n:
                u = dot(inv, s_v[lo:hi, hi:], HIGHEST)
                s_v[hi:, hi:] = s_v[hi:, hi:] - dot_t(u, u, HIGHEST)
                m_v[hi:, :hi] = m_v[hi:, :hi] - dot_t(u, m_v[lo:hi, :hi], HIGHEST)
            run(queue, share)
        run(queue, len(queue))
        project(0, width, False)
        project(width, width + half, False)
        for h in range(2):
            for up, other in pieces[h]:
                up.wait_send()
        for b in range(blocks):
            for up, _ in mpieces[b]:
                up.wait_send()
        side.wait_send()

    @pl.when(later)
    def _():
        m_v[:half, half:width] = jnp.zeros((half, half), jnp.float32)
        for p in pieces[0]:
            forward(p)
        for c in loads:
            c.wait()
        for up, side in pieces[0]:
            side.wait_recv()
        for l in range(nbl):
            multiply(0, l)
            begin(units[0][l])
        queue = wave(units[0])
        for i, p in enumerate(pieces[1]):
            forward(p)
            run(queue, nbl - 1)
        for up, side in pieces[1]:
            side.wait_recv()
        for l in range(nbl):
            multiply(1, l)
            begin(units[1][l])
            run(queue, 1)
        run(queue, len(queue))
        queue = wave(units[1])
        run(queue, nbl * bits)
        for p in mpieces[0]:
            forward(p)
        run(queue, nbl)
        for p in mpieces[1]:
            forward(p)
        run(queue, len(queue))
        @pl.when(inner)
        def _():
            for p in mpieces[2] + mpieces[3]:
                forward(p)

        for b in range(2):
            for up, side in mpieces[b]:
                side.wait_recv()
        project(0, width, False)

        @pl.when(last)
        def _():
            for p in mpieces[2]:
                forward(p)

        for up, side in mpieces[2]:
            side.wait_recv()
        project(width, width + half, False)

        @pl.when(last)
        def _():
            for p in mpieces[3]:
                forward(p)

        for up, side in mpieces[3]:
            side.wait_recv()
        for group in mpieces:
            for up, side in group:
                side.wait_send()

        @pl.when(inner)
        def _():
            for group in pieces + mpieces:
                for up, side in group:
                    up.wait_send()

    project(width + half, n, True)
    for h in range(2):
        for up, side in pieces[h]:
            side.wait_send()
        for unit in units[h]:
            for s, down, up in unit[2]:
                for d in down:
                    d[0].wait_send()
                for c in up:
                    c.wait_send()
    for c in outs + list(couts.values()):
        c.wait()


def solution(mesh):
    rows_n, cols_n = mesh.shape["row"], mesh.shape["col"]
    bits = rows_n.bit_length() - 1

    def on_device(matrix):
        count, nbl, width = matrix.shape
        half, n = width // 2, 2 * width
        units = 2 * nbl
        f32 = jnp.float32
        dma = pltpu.SemaphoreType.DMA
        anywhere = pl.BlockSpec(memory_space=pl.ANY)
        return pl.pallas_call(
            functools.partial(qr_kernel, rows_n, cols_n),
            out_shape=(
                jax.ShapeDtypeStruct((n, nbl, width), f32),
                jax.ShapeDtypeStruct((count, nbl, width), f32),
            ),
            in_specs=[anywhere],
            out_specs=(anywhere, anywhere),
            scratch_shapes=[
                pltpu.VMEM((nbl, count, width), f32),
                pltpu.VMEM((n // half, count, half), f32),
                pltpu.VMEM((n, nbl * width), f32),
                pltpu.VMEM((n, nbl * width), f32),
                pltpu.VMEM((units, 2, half, width), f32),
                pltpu.VMEM((2, n, width), f32),
                pltpu.VMEM((n, n), f32),
                pltpu.VMEM((n, n), f32),
                pltpu.VMEM((half, width), f32),
                pltpu.VMEM((half, width), f32),
                pltpu.VMEM((nbl, n, width), f32),
                dma((nbl,)),
                dma((2,)),
                dma((3 * nbl,)),
                dma((nbl,)),
            ]
            + [dma((2 * PIECES,))] * 4
            + [dma((2 * n // half,))] * 4
            + [dma((1,))] * 2
            + [dma((units, 2, bits))] * 4,
            compiler_params=pltpu.CompilerParams(
                collective_id=0, has_side_effects=True, vmem_limit_bytes=48 * 1024 * 1024
            ),
            name="block_qr",
        )(matrix)

    return jax.shard_map(
        on_device,
        mesh=mesh,
        in_specs=(P("row", None, "col"),),
        out_specs=(P(None, None, "col"), P("row", None, "col")),
        check_vma=False,
    )
```
